512 devices in a mesh: row: 16 (over z_hi, x, core), col: 4 (over y), depth: 8 (over z_lo).
Axes of the slice: x: 4, y: 4, z: 16 (z_hi: 2, z_lo: 8; z = z_hi * 8 + z_lo), core: 2. Of those that a mesh axis runs over, the one named last changes fastest.
Arguments:
- activations: bfloat16 [16384, 4544], P(('depth', 'row'), 'col'), may hold values from -6 to 6
- out_grads: bfloat16 [16384, 12288], P(('depth', 'col'), 'row'), may hold values from -0.09375 to 0.09375
Outputs:
- weight_grad: float32 [12288, 4544], P(('row', 'depth'), 'col')
The draws below stay inside these ranges and needn't reach their ends.
All inputs are finite; a program needn't handle non-finite values.
Results may differ from the reference program's by a relative error of at most 0.0003.
Values may be sent and summed in bfloat16 or wider, within the bound.
No kernel may reach another device: no remote copies, remote signals or barrier semaphores. Data moves between devices by JAX's collectives and lax.ppermute only.
A program may use at most 64 MiB of HBM per device.

```python
import jax
import jax.numpy as jnp
from jax import lax

D = 4544
FFW = 12288
TOKENS = 16384


def raised(result, rng, source, target, parts, factor):
    owner, partner = [(jnp.arange(result.shape[dim]) // (result.shape[dim] // parts)).reshape([-1 if axis == dim else 1 for axis in range(result.ndim)]) for dim in (source, target)]
    chosen = jax.random.permutation(rng, parts)[partner]
    strong = (owner == chosen) | (owner == (partner + parts // 2) % parts)
    return jnp.where(strong, factor * result, result)


def steps_of(stream_key, shape, split, low, top_value):
    gain = 1.0
    for axis_at, shards_of in split:
        heights = jax.random.uniform(jax.random.fold_in(jax.random.fold_in(stream_key, 6), axis_at), (shards_of,), jnp.float32, low / len(split), top_value / len(split))
        gain = gain * jnp.repeat(jnp.exp(heights), shape[axis_at] // shards_of).reshape((-1,) + (1,) * (len(shape) - 1 - axis_at))
    return gain


def scatter_about(stream_key, extent, scale, bound, shards=(), dtype=jnp.bfloat16):
    array = jax.random.normal(stream_key, extent, jnp.float32) * scale
    if len(shards) > 0:
        array = steps_of(stream_key, extent, shards, -0.22, 0.18) * array
    return jnp.clip(array, min=-bound, max=bound).astype(dtype)


def bell_draw_with(key, extent, width, most, shards, heavy, kind=jnp.bfloat16):
    result = width * jax.random.normal(key, extent, jnp.float32)
    if shards:
        result = result * steps_of(key, extent, shards, -0.22, 0.18)
    return jnp.clip(raised(result, jax.random.fold_in(key, 3), *heavy), -most, most).astype(kind)


def setup_inputs(seed: int = 0) -> dict:
    key_of = jax.random.split(jax.random.key(seed), 3)
    activations = scatter_about(key_of[0], (TOKENS, D), 1.0, 6.0, ((0, 128), (1, 4)))
    out_grads = bell_draw_with(key_of[1], (TOKENS, FFW), TOKENS ** -0.5, 0.09375, ((0, 32), (1, 16)), (0, 1, 32, 2.75))
    return dict(activations=activations, out_grads=out_grads)


def reference(activations, out_grads):
    return lax.dot_general(out_grads, activations, (((0,), (0,)), ((), ())), preferred_element_type=jnp.float32)
```

```python
import functools
import jax
import jax.numpy as jnp
from jax import lax
from jax.experimental import pallas as pl
from jax.experimental.pallas import tpu as pltpu
from jax.sharding import PartitionSpec as P

AXES = ("row", "col", "depth")
SIZES = (2, 4, 2, 4, 8)


def permute(value, target):
    pairs = []
    for zh in range(2):
        for x in range(4):
            for core in range(2):
                for y in range(4):
                    for zl in range(8):
                        to = target(zh, x, core, y, zl)
                        if to is not None:
                            flat = lambda c: ((((c[0] * 4 + c[1]) * 2 + c[2]) * 4 + c[3]) * 8 + c[4])
                            pairs.append((flat((zh, x, core, y, zl)), flat(to)))
    return lax.ppermute(value, AXES, pairs)


def over_x(value, step):
    return permute(value, lambda zh, x, c, y, zl: (zh, (x - step) % 4, c, y, zl))


def over_y(value, step):
    return permute(value, lambda zh, x, c, y, zl: (zh, x, c, (y - step) % 4, zl))


def other_core(value):
    return permute(value, lambda zh, x, c, y, zl: (zh, x, 1 - c, y, zl))


def other_half(value):
    return permute(value, lambda zh, x, c, y, zl: (1 - zh, x, c, y, zl))


def other_quad(value):
    return permute(value, lambda zh, x, c, y, zl: (zh, x, c, y, zl ^ 4))


def depth_pair(value, bit):
    return permute(value, lambda zh, x, c, y, zl: (zh, x, c, y, zl ^ bit))


NT = (((1,), (1,)), ((), ()))
TILES = ((0, 256), (256, 512), (512, 768), (768, 1024), (1024, 1136))
f16, f32, bf16 = jnp.float16, jnp.float32, jnp.bfloat16
PARAMS = pltpu.CompilerParams(vmem_limit_bytes=40 * 2**20)
VM = pl.BlockSpec(memory_space=pltpu.VMEM)
SM = pl.BlockSpec(memory_space=pltpu.SMEM)
ANY = pl.BlockSpec(memory_space=pl.ANY)


def cost(us):
    return pl.CostEstimate(flops=int(us * 1e9), bytes_accessed=2**20, transcendentals=0)


def shape(dims, dtype):
    return jax.ShapeDtypeStruct(dims, dtype)


def tie(*values):
    return lax.optimization_barrier(values)


def lanes_at(start, size):
    return pl.ds(pl.multiple_of(start, 128), size)


def fence_kernel(ref, out_ref):
    out_ref[...] = ref[...]


def prep_kernel(at_ref, all_ref, grads_ref, fetched, turned, sems):
    zh, zl = at_ref[0], at_ref[4]
    b0, b1, quad = lax.rem(zl, 2), lax.rem(zl // 2, 2), zl // 4
    copies = [pltpu.make_async_copy(all_ref.at[pl.ds(j * 512, 512), :], fetched.at[j], sems.at[j]) for j in range(4)]
    for copy in copies:
        copy.start()
    for j, copy in enumerate(copies):
        copy.wait()
        turned[...] = fetched[j].T
        slot = lax.rem(j - 2 * zh + 4, 4)
        for k in range(8):
            owner_quad = 1 - quad if k < 4 else quad
            owner_b0 = 1 - b0 if k % 4 < 2 else b0
            owner_b1 = 1 - b1 if k % 2 == 0 else b1
            first = (owner_quad * 4 + owner_b1 * 2 + owner_b0) * 96
            grads_ref[slot, k * 96:(k + 1) * 96, :] = turned[pl.ds(pl.multiple_of(first, 32), 96), :]


def spread(at_ref, own, other, acts_ref, sems):
    x, core = at_ref[1], at_ref[2]
    copies = []
    for xr in range(4):
        slot = lax.rem(x + xr, 4) * 256
        for i, (src, c) in enumerate(((own, core), (other, 1 - core))):
            copies.append(pltpu.make_async_copy(src.at[xr], acts_ref.at[:, lanes_at(slot + c * 128, 128)], sems.at[2 * xr + i]))
    for copy in copies:
        copy.start()
    return copies


def own_kernel(at_ref, s0, t0, grads_ref, token, out_ref, acts_ref, sems):
    for copy in spread(at_ref, s0, t0, acts_ref, sems):
        copy.wait()
    for lo, hi in TILES:
        out_ref[:, lo:hi] = sum(
            lax.dot_general(grads_ref[j], acts_ref[lo:hi, j * 512:(j + 1) * 512], NT, preferred_element_type=f32) for j in range(2))


def rest_kernel(at_ref, s1, t1, grads_ref, start_ref, far_ref, near_ref, keep_far_ref, keep_near_ref, acts_ref, sems):
    for copy in spread(at_ref, s1, t1, acts_ref, sems):
        copy.wait()
    top = None
    for lo, hi in TILES:
        part = start_ref[:, lo:hi] + sum(
            lax.dot_general(grads_ref[2 + j], acts_ref[lo:hi, j * 512:(j + 1) * 512], NT, preferred_element_type=f32) for j in range(2))
        far_ref[:, lo:hi] = part[:192]
        keep_far_ref[:, lo:hi] = part[192:384]
        near_ref[:, lo:hi] = part[384:576]
        keep_near_ref[:, lo:hi] = part[576:]
        part = jnp.max(jnp.abs(part), axis=0, keepdims=True)
        part = jnp.max(part, axis=1, keepdims=True)
        top = part if top is None else jnp.maximum(top, part)
    size = jnp.clip(jnp.ceil(jnp.log2(top)) + 1, -100, 100)
    scale = jnp.exp2(15 - size)
    for ref in (far_ref, near_ref):
        ref[:, :1136] = ref[:, :1136] * scale
    for ref in (far_ref, near_ref, keep_far_ref, keep_near_ref):
        ref[:, 1136:] = jnp.broadcast_to(size, (192, 16))


def add(keep, message):
    message = message.astype(f32)
    size = message[:, 1136:1137]
    total = keep + message * jnp.exp2(size - 15)
    return total, jnp.maximum(keep[:, 1136:1137], size) + 1


def tagged(total, size, scale):
    return jnp.where(lax.broadcasted_iota(jnp.int32, total.shape, 1) < 1136, total * scale, size)


def wrap(total, size):
    return tagged(total, size, jnp.exp2(15 - size)).astype(f16)


def again(token):
    return pl.pallas_call(
        fence_kernel, out_shape=shape((8, 128), f32), in_specs=[VM], out_specs=VM, compiler_params=PARAMS, name="fence",
    )(token)


def body(activations, out_grads):
    row, y, zl = (lax.axis_index(a) for a in AXES)
    where = jnp.stack([row // 8, row // 2 % 4, row % 2, y, zl]).astype(jnp.int32)
    bt = activations.T
    token = again(jnp.zeros((8, 128), f32) + row.astype(f32))
    every_grad = lax.all_gather(out_grads, "col", axis=0, tiled=True)
    bt, token = tie(bt, token)
    swapped = other_half(bt)
    x1, x2, x3 = (over_x(bt, s) for s in (1, 2, 3))
    swapped, token = tie(swapped, token)
    token = again(token)
    x1, x2, x3, swapped, token = tie(x1, x2, x3, swapped, token)
    s0 = jnp.stack([bt, x1, x2, x3])
    t0 = other_core(s0)
    o1, o2, o3 = (over_x(swapped, s) for s in (1, 2, 3))
    grads = pl.pallas_call(
        prep_kernel, out_shape=shape((4, 768, 512), bf16),
        in_specs=[SM, ANY], out_specs=VM, compiler_params=PARAMS, name="prep",
        scratch_shapes=[pltpu.VMEM((4, 512, 768), bf16), pltpu.VMEM((768, 512), bf16), pltpu.SemaphoreType.DMA((4,))],
    )(where, every_grad)
    o1, o2, o3, grads = tie(o1, o2, o3, grads)
    s1 = jnp.stack([swapped, o1, o2, o3])
    t1 = other_core(s1)
    t0, s1 = tie(t0, s1)
    start = pl.pallas_call(
        own_kernel, out_shape=shape((768, 1136), f32),
        in_specs=[SM] + [ANY] * 2 + [VM] * 2, out_specs=VM, compiler_params=PARAMS, name="own",
        scratch_shapes=[pltpu.VMEM((1136, 1024), bf16), pltpu.SemaphoreType.DMA((8,))],
    )(where, s0, t0, grads, token)
    t1, start = tie(t1, start)
    far, near, keep_far, keep_near = pl.pallas_call(
        rest_kernel, out_shape=(shape((192, 1152), f32),) * 4,
        in_specs=[SM] + [ANY] * 2 + [VM] * 2, out_specs=(VM,) * 4, compiler_params=PARAMS, name="rest",
        scratch_shapes=[pltpu.VMEM((1136, 1024), bf16), pltpu.SemaphoreType.DMA((8,))],
    )(where, s1, t1, grads, start)
    f1, n1 = depth_pair(far.astype(f16), 1), depth_pair(near.astype(f16), 1)
    far, size = add(keep_far, f1)
    f2 = depth_pair(wrap(far[:96], size[:96]), 2)
    n1, far = tie(n1, tagged(far[96:], size[96:], 1))
    near, size = add(keep_near, n1)
    n2 = depth_pair(wrap(near[:96], size[:96]), 2)
    crossed = depth_pair(wrap(*add(far, f2)), 4)
    near, size = add(tagged(near[96:], size[96:], 1), n2)
    near, crossed = tie(tagged(near, size, 1), crossed)
    return add(near, crossed)[0][:, :1136]


def solution(mesh):
    in_specs = (P(("depth", "row"), "col"), P(("depth", "col"), "row"))
    out_specs = P(("row", "depth"), "col")
    return jax.shard_map(body, mesh=mesh, in_specs=in_specs, out_specs=out_specs, check_vma=False)
```

```python
import functools
import jax
import jax.numpy as jnp
from jax import lax
from jax.experimental import pallas as pl
from jax.experimental.pallas import tpu as pltpu
from jax.sharding import PartitionSpec as P

AXES = ("row", "col", "depth")
SIZES = (2, 4, 2, 4, 8)


def permute(value, target):
    pairs = []
    for zh in range(2):
        for x in range(4):
            for core in range(2):
                for y in range(4):
                    for zl in range(8):
                        to = target(zh, x, core, y, zl)
                        if to is not None:
                            flat = lambda c: ((((c[0] * 4 + c[1]) * 2 + c[2]) * 4 + c[3]) * 8 + c[4])
                            pairs.append((flat((zh, x, core, y, zl)), flat(to)))
    return lax.ppermute(value, AXES, pairs)


def over_x(value, step):
    return permute(value, lambda zh, x, c, y, zl: (zh, (x - step) % 4, c, y, zl))


def over_y(value, step):
    return permute(value, lambda zh, x, c, y, zl: (zh, x, c, (y - step) % 4, zl))


def other_core(value):
    return permute(value, lambda zh, x, c, y, zl: (zh, x, 1 - c, y, zl))


def other_half(value):
    return permute(value, lambda zh, x, c, y, zl: (1 - zh, x, c, y, zl))


def other_quad(value):
    return permute(value, lambda zh, x, c, y, zl: (zh, x, c, y, zl ^ 4))


def depth_pair(value, bit):
    return permute(value, lambda zh, x, c, y, zl: (zh, x, c, y, zl ^ bit))


NT = (((1,), (1,)), ((), ()))
TILES = ((0, 256), (256, 512), (512, 768), (768, 1024), (1024, 1136))
f16, f32, bf16 = jnp.float16, jnp.float32, jnp.bfloat16
PARAMS = pltpu.CompilerParams(vmem_limit_bytes=40 * 2**20)
VM = pl.BlockSpec(memory_space=pltpu.VMEM)
SM = pl.BlockSpec(memory_space=pltpu.SMEM)
ANY = pl.BlockSpec(memory_space=pl.ANY)


def cost(us):
    return pl.CostEstimate(flops=int(us * 1e9), bytes_accessed=2**20, transcendentals=0)


def shape(dims, dtype):
    return jax.ShapeDtypeStruct(dims, dtype)


def tie(*values):
    return lax.optimization_barrier(values)


def lanes_at(start, size):
    return pl.ds(pl.multiple_of(start, 128), size)


def fence_kernel(ref, out_ref):
    out_ref[...] = ref[...]


def prep_kernel(at_ref, all_ref, grads_ref, fetched, turned, sems):
    zh, zl = at_ref[0], at_ref[4]
    b0, b1, quad = lax.rem(zl, 2), lax.rem(zl // 2, 2), zl // 4
    copies = [pltpu.make_async_copy(all_ref.at[pl.ds(j * 512, 512), :], fetched.at[j], sems.at[j]) for j in range(4)]
    for copy in copies:
        copy.start()
    for j, copy in enumerate(copies):
        copy.wait()
        turned[...] = fetched[j].T
        slot = lax.rem(j - 2 * zh + 4, 4)
        for k in range(8):
            owner_quad = 1 - quad if k < 4 else quad
            owner_b0 = 1 - b0 if k % 4 < 2 else b0
            owner_b1 = 1 - b1 if k % 2 == 0 else b1
            first = (owner_quad * 4 + owner_b1 * 2 + owner_b0) * 96
            grads_ref[slot, k * 96:(k + 1) * 96, :] = turned[pl.ds(pl.multiple_of(first, 32), 96), :]


def spread(at_ref, own, other, acts_ref, sems):
    x, core = at_ref[1], at_ref[2]
    copies = []
    for xr in range(4):
        slot = lax.rem(x + xr, 4) * 256
        for i, (src, c) in enumerate(((own, core), (other, 1 - core))):
            copies.append(pltpu.make_async_copy(src.at[xr], acts_ref.at[:, lanes_at(slot + c * 128, 128)], sems.at[2 * xr + i]))
    for copy in copies:
        copy.start()
    return copies


def own_kernel(at_ref, s0, t0, grads_ref, token, out_ref, acts_ref, sems):
    for copy in spread(at_ref, s0, t0, acts_ref, sems):
        copy.wait()
    for lo, hi in TILES:
        out_ref[:, lo:hi] = sum(
            lax.dot_general(grads_ref[j], acts_ref[lo:hi, j * 512:(j + 1) * 512], NT, preferred_element_type=f32) for j in range(2))


def rest_kernel(at_ref, s1, t1, grads_ref, start_ref, *refs):
    far0_ref, far1_ref, near0_ref, near1_ref, keep_far_ref, keep_near_ref, acts_ref, sems = refs
    for copy in spread(at_ref, s1, t1, acts_ref, sems):
        copy.wait()
    sends = (far0_ref, far1_ref, near0_ref, near1_ref)
    top = None
    for lo, hi in TILES:
        part = start_ref[:, lo:hi] + sum(
            lax.dot_general(grads_ref[2 + j], acts_ref[lo:hi, j * 512:(j + 1) * 512], NT, preferred_element_type=f32) for j in range(2))
        for ref, first in zip(sends, (0, 96, 384, 480)):
            ref[:, lo:hi] = part[first:first + 96]
        keep_far_ref[:, lo:hi] = part[192:384]
        keep_near_ref[:, lo:hi] = part[576:]
        part = jnp.max(jnp.abs(part), axis=0, keepdims=True)
        part = jnp.max(part, axis=1, keepdims=True)
        top = part if top is None else jnp.maximum(top, part)
    size = jnp.clip(jnp.ceil(jnp.log2(top)) + 1, -100, 100)
    scale = jnp.exp2(15 - size)
    for ref in sends:
        ref[:, :1136] = ref[:, :1136] * scale
    for ref in (*sends, keep_far_ref, keep_near_ref):
        ref[:, 1136:] = jnp.broadcast_to(size, (ref.shape[0], 16))


def stage_kernel(spans, keep_ref, message_ref, *out_refs):
    message = message_ref[...]
    size = message[:, 1136:1137]
    total = keep_ref[...] + message * jnp.exp2(size - 15)
    size = jnp.maximum(keep_ref[:, 1136:1137], size) + 1
    lane = lax.broadcasted_iota(jnp.int32, total.shape, 1)
    kept = jnp.where(lane < 1136, total, size)
    sent = jnp.where(lane < 1136, total * jnp.exp2(15 - size), size)
    for (first, rows, scaled), ref in zip(spans, out_refs):
        ref[...] = (sent if scaled else kept)[first:first + rows]


def stage(keep, message, *spans):
    return pl.pallas_call(
        functools.partial(stage_kernel, spans), out_shape=tuple(shape((rows, 1152), f32) for _, rows, _ in spans),
        in_specs=[VM] * 2, out_specs=(VM,) * len(spans), compiler_params=PARAMS, name="stage",
    )(keep, message.astype(f32))


def final_kernel(n0_ref, n1_ref, c0_ref, c1_ref, out_ref):
    messages = []
    for ref in (c0_ref, c1_ref):
        message = ref[...]
        messages.append(message * jnp.exp2(message[:, 1136:1137] - 15))
    near = jnp.concatenate([n0_ref[...], n1_ref[...]], axis=0)
    out_ref[...] = (near + jnp.concatenate(messages, axis=0))[:, :1136]


def again(token):
    return pl.pallas_call(
        fence_kernel, out_shape=shape((8, 128), f32), in_specs=[VM], out_specs=VM, compiler_params=PARAMS, name="fence",
    )(token)


FIRST = 64


def body(activations, out_grads):
    row, y, zl = (lax.axis_index(a) for a in AXES)
    where = jnp.stack([row // 8, row // 2 % 4, row % 2, y, zl]).astype(jnp.int32)
    bt = activations.T
    token = again(jnp.zeros((8, 128), f32) + row.astype(f32))
    every_grad = lax.all_gather(out_grads, "col", axis=0, tiled=True)
    bt, token = tie(bt, token)
    swapped = other_half(bt)
    x1, x2, x3 = (over_x(bt, s) for s in (1, 2, 3))
    swapped, token = tie(swapped, token)
    token = again(token)
    x1, x2, x3, swapped, token = tie(x1, x2, x3, swapped, token)
    s0 = jnp.stack([bt, x1, x2, x3])
    t0 = other_core(s0)
    o1, o2, o3 = (over_x(swapped, s) for s in (1, 2, 3))
    grads = pl.pallas_call(
        prep_kernel, out_shape=shape((4, 768, 512), bf16),
        in_specs=[SM, ANY], out_specs=VM, compiler_params=PARAMS, name="prep",
        scratch_shapes=[pltpu.VMEM((4, 512, 768), bf16), pltpu.VMEM((768, 512), bf16), pltpu.SemaphoreType.DMA((4,))],
    )(where, every_grad)
    o1, o2, o3, grads = tie(o1, o2, o3, grads)
    s1 = jnp.stack([swapped, o1, o2, o3])
    t1 = other_core(s1)
    t0, s1 = tie(t0, s1)
    start = pl.pallas_call(
        own_kernel, out_shape=shape((768, 1136), f32),
        in_specs=[SM] + [ANY] * 2 + [VM] * 2, out_specs=VM, compiler_params=PARAMS, name="own",
        scratch_shapes=[pltpu.VMEM((1136, 1024), bf16), pltpu.SemaphoreType.DMA((8,))],
    )(where, s0, t0, grads, token)
    t1, start = tie(t1, start)
    *sends, keep_far, keep_near = pl.pallas_call(
        rest_kernel, out_shape=(shape((96, 1152), f32),) * 4 + (shape((192, 1152), f32),) * 2,
        in_specs=[SM] + [ANY] * 2 + [VM] * 2, out_specs=(VM,) * 6, compiler_params=PARAMS, name="rest",
        scratch_shapes=[pltpu.VMEM((1136, 1024), bf16), pltpu.SemaphoreType.DMA((8,))],
    )(where, s1, t1, grads, start)
    f0, f1, n0, n1 = (depth_pair(m.astype(f16), 1) for m in sends)
    f2 = stage(keep_far[:96], f0, (0, FIRST, True), (FIRST, 96 - FIRST, True))
    f2 = [depth_pair(m.astype(f16), 2) for m in f2]
    k0, k1 = stage(keep_far[96:], f1, (0, FIRST, False), (FIRST, 96 - FIRST, False))
    n2 = stage(keep_near[:96], n0, (0, 48, True), (48, 48, True))
    n2 = [depth_pair(m.astype(f16), 2) for m in n2]
    crossed = [depth_pair(stage(k, m, (0, k.shape[0], True))[0].astype(f16), 4) for k, m in zip((k0, k1), f2)]
    n0, n1 = stage(keep_near[96:], n1, (0, 48, False), (48, 48, False))
    near = [stage(k, m, (0, 48, False))[0] for k, m in zip((n0, n1), n2)]
    *near, c0, c1 = tie(*near, *crossed)
    return pl.pallas_call(
        final_kernel, out_shape=shape((96, 1136), f32), in_specs=[VM] * 4, out_specs=VM, compiler_params=PARAMS, name="final",
    )(*near, c0.astype(f32), c1.astype(f32))


def solution(mesh):
    in_specs = (P(("depth", "row"), "col"), P(("depth", "col"), "row"))
    out_specs = P(("row", "depth"), "col")
    return jax.shard_map(body, mesh=mesh, in_specs=in_specs, out_specs=out_specs, check_vma=False)
```

```python
import functools
import jax
import jax.numpy as jnp
from jax import lax
from jax.experimental import pallas as pl
from jax.experimental.pallas import tpu as pltpu
from jax.sharding import PartitionSpec as P

AXES = ("row", "col", "depth")
SIZES = (2, 4, 2, 4, 8)


def permute(value, target):
    pairs = []
    for zh in range(2):
        for x in range(4):
            for core in range(2):
                for y in range(4):
                    for zl in range(8):
                        to = target(zh, x, core, y, zl)
                        if to is not None:
                            flat = lambda c: ((((c[0] * 4 + c[1]) * 2 + c[2]) * 4 + c[3]) * 8 + c[4])
                            pairs.append((flat((zh, x, core, y, zl)), flat(to)))
    return lax.ppermute(value, AXES, pairs)


def over_x(value, step):
    return permute(value, lambda zh, x, c, y, zl: (zh, (x - step) % 4, c, y, zl))


def over_y(value, step):
    return permute(value, lambda zh, x, c, y, zl: (zh, x, c, (y - step) % 4, zl))


def other_core(value):
    return permute(value, lambda zh, x, c, y, zl: (zh, x, 1 - c, y, zl))


def other_half(value):
    return permute(value, lambda zh, x, c, y, zl: (1 - zh, x, c, y, zl))


def other_quad(value):
    return permute(value, lambda zh, x, c, y, zl: (zh, x, c, y, zl ^ 4))


def depth_pair(value, bit):
    return permute(value, lambda zh, x, c, y, zl: (zh, x, c, y, zl ^ bit))


NT = (((1,), (1,)), ((), ()))
TILES = ((0, 256), (256, 512), (512, 768), (768, 1024), (1024, 1136))
f16, f32, bf16 = jnp.float16, jnp.float32, jnp.bfloat16
PARAMS = pltpu.CompilerParams(vmem_limit_bytes=40 * 2**20)
VM = pl.BlockSpec(memory_space=pltpu.VMEM)
SM = pl.BlockSpec(memory_space=pltpu.SMEM)
ANY = pl.BlockSpec(memory_space=pl.ANY)


def cost(us):
    return pl.CostEstimate(flops=int(us * 1e9), bytes_accessed=2**20, transcendentals=0)


def shape(dims, dtype):
    return jax.ShapeDtypeStruct(dims, dtype)


def tie(*values):
    return lax.optimization_barrier(values)


def lanes_at(start, size):
    return pl.ds(pl.multiple_of(start, 128), size)


def fence_kernel(ref, out_ref):
    out_ref[...] = ref[...]


def prep_kernel(at_ref, all_ref, grads_ref, fetched, turned, sems):
    zh, zl = at_ref[0], at_ref[4]
    b0, b1, quad = lax.rem(zl, 2), lax.rem(zl // 2, 2), zl // 4
    copies = [pltpu.make_async_copy(all_ref.at[pl.ds(j * 512, 512), :], fetched.at[j], sems.at[j]) for j in range(4)]
    for copy in copies:
        copy.start()
    for j, copy in enumerate(copies):
        copy.wait()
        turned[...] = fetched[j].T
        slot = lax.rem(j - 2 * zh + 4, 4)
        for k in range(8):
            owner_quad = 1 - quad if k < 4 else quad
            owner_b0 = 1 - b0 if k % 4 < 2 else b0
            owner_b1 = 1 - b1 if k % 2 == 0 else b1
            first = (owner_quad * 4 + owner_b1 * 2 + owner_b0) * 96
            grads_ref[slot, k * 96:(k + 1) * 96, :] = turned[pl.ds(pl.multiple_of(first, 32), 96), :]


def spread(at_ref, own, other, acts_ref, sems):
    x, core = at_ref[1], at_ref[2]
    copies = []
    for xr in range(4):
        slot = lax.rem(x + xr, 4) * 256
        for i, (src, c) in enumerate(((own, core), (other, 1 - core))):
            copies.append(pltpu.make_async_copy(src.at[xr], acts_ref.at[:, lanes_at(slot + c * 128, 128)], sems.at[2 * xr + i]))
    for copy in copies:
        copy.start()
    return copies


def own_kernel(at_ref, s0, t0, grads_ref, token, out_ref, acts_ref, sems):
    for copy in spread(at_ref, s0, t0, acts_ref, sems):
        copy.wait()
    for lo, hi in TILES:
        out_ref[:, lo:hi] = sum(
            lax.dot_general(grads_ref[j], acts_ref[lo:hi, j * 512:(j + 1) * 512], NT, preferred_element_type=f32) for j in range(2))


def rest_kernel(at_ref, s1, t1, grads_ref, start_ref, *refs):
    far0_ref, far1_ref, near0_ref, near1_ref, keep_far_ref, keep_near_ref, acts_ref, sems = refs
    for copy in spread(at_ref, s1, t1, acts_ref, sems):
        copy.wait()
    sends = (far0_ref, far1_ref, near0_ref, near1_ref)
    top = None
    for lo, hi in TILES:
        part = start_ref[:, lo:hi] + sum(
            lax.dot_general(grads_ref[2 + j], acts_ref[lo:hi, j * 512:(j + 1) * 512], NT, preferred_element_type=f32) for j in range(2))
        for ref, first in zip(sends, (0, 96, 384, 480)):
            ref[:, lo:hi] = part[first:first + 96]
        keep_far_ref[:, lo:hi] = part[192:384]
        keep_near_ref[:, lo:hi] = part[576:]
        part = jnp.max(jnp.abs(part), axis=0, keepdims=True)
        part = jnp.max(part, axis=1, keepdims=True)
        top = part if top is None else jnp.maximum(top, part)
    size = jnp.clip(jnp.ceil(jnp.log2(top)) + 1, -100, 100)
    scale = jnp.exp2(15 - size)
    for ref in sends:
        ref[:, :1136] = ref[:, :1136] * scale
    for ref in (*sends, keep_far_ref, keep_near_ref):
        ref[:, 1136:] = jnp.broadcast_to(size, (ref.shape[0], 16))


def stage_kernel(spans, keep_ref, message_ref, *out_refs):
    message = message_ref[...]
    size = message[:, 1136:1137]
    total = keep_ref[...] + message * jnp.exp2(size - 15)
    size = jnp.maximum(keep_ref[:, 1136:1137], size) + 1
    lane = lax.broadcasted_iota(jnp.int32, total.shape, 1)
    kept = jnp.where(lane < 1136, total, size)
    sent = jnp.where(lane < 1136, total * jnp.exp2(15 - size), size)
    for (first, rows, scaled), ref in zip(spans, out_refs):
        ref[...] = (sent if scaled else kept)[first:first + rows]


def stage(keep, message, *spans):
    return pl.pallas_call(
        functools.partial(stage_kernel, spans), out_shape=tuple(shape((rows, 1152), f32) for _, rows, _ in spans),
        in_specs=[VM] * 2, out_specs=(VM,) * len(spans), compiler_params=PARAMS, name="stage",
    )(keep, message.astype(f32))


def final_kernel(near_ref, message_ref, out_ref):
    message = message_ref[...]
    out_ref[...] = (near_ref[...] + message * jnp.exp2(message[:, 1136:1137] - 15))[:, :1136]


def again(token):
    return pl.pallas_call(
        fence_kernel, out_shape=shape((8, 128), f32), in_specs=[VM], out_specs=VM, compiler_params=PARAMS, name="fence",
    )(token)


FIRST = 64


def body(activations, out_grads):
    row, y, zl = (lax.axis_index(a) for a in AXES)
    where = jnp.stack([row // 8, row // 2 % 4, row % 2, y, zl]).astype(jnp.int32)
    bt = activations.T
    token = again(jnp.zeros((8, 128), f32) + row.astype(f32))
    every_grad = lax.all_gather(out_grads, "col", axis=0, tiled=True)
    bt, token = tie(bt, token)
    swapped = other_half(bt)
    x1, x2, x3 = (over_x(bt, s) for s in (1, 2, 3))
    swapped, token = tie(swapped, token)
    token = again(token)
    x1, x2, x3, swapped, token = tie(x1, x2, x3, swapped, token)
    s0 = jnp.stack([bt, x1, x2, x3])
    t0 = other_core(s0)
    o1, o2, o3 = (over_x(swapped, s) for s in (1, 2, 3))
    grads = pl.pallas_call(
        prep_kernel, out_shape=shape((4, 768, 512), bf16),
        in_specs=[SM, ANY], out_specs=VM, compiler_params=PARAMS, name="prep",
        scratch_shapes=[pltpu.VMEM((4, 512, 768), bf16), pltpu.VMEM((768, 512), bf16), pltpu.SemaphoreType.DMA((4,))],
    )(where, every_grad)
    o1, o2, o3, grads = tie(o1, o2, o3, grads)
    s1 = jnp.stack([swapped, o1, o2, o3])
    t1 = other_core(s1)
    t0, s1 = tie(t0, s1)
    start = pl.pallas_call(
        own_kernel, out_shape=shape((768, 1136), f32),
        in_specs=[SM] + [ANY] * 2 + [VM] * 2, out_specs=VM, compiler_params=PARAMS, name="own",
        scratch_shapes=[pltpu.VMEM((1136, 1024), bf16), pltpu.SemaphoreType.DMA((8,))],
    )(where, s0, t0, grads, token)
    t1, start = tie(t1, start)
    *sends, keep_far, keep_near = pl.pallas_call(
        rest_kernel, out_shape=(shape((96, 1152), f32),) * 4 + (shape((192, 1152), f32),) * 2,
        in_specs=[SM] + [ANY] * 2 + [VM] * 2, out_specs=(VM,) * 6, compiler_params=PARAMS, name="rest",
        scratch_shapes=[pltpu.VMEM((1136, 1024), bf16), pltpu.SemaphoreType.DMA((8,))],
    )(where, s1, t1, grads, start)
    f0, f1, n0, n1 = (depth_pair(m.astype(f16), 1) for m in sends)
    (f2,) = stage(keep_far[:96], f0, (0, 96, True))
    f2 = depth_pair(f2.astype(f16), 2)
    (far,) = stage(keep_far[96:], f1, (0, 96, False))
    (n2,) = stage(keep_near[:96], n0, (0, 96, True))
    n2 = depth_pair(n2.astype(f16), 2)
    crossed = depth_pair(stage(far, f2, (0, 96, True))[0].astype(f16), 4)
    (near,) = stage(keep_near[96:], n1, (0, 96, False))
    (near,) = stage(near, n2, (0, 96, False))
    near, crossed = tie(near, crossed)
    return pl.pallas_call(
        final_kernel, out_shape=shape((96, 1136), f32), in_specs=[VM] * 2, out_specs=VM, compiler_params=PARAMS, name="final",
    )(near, crossed.astype(f32))


def solution(mesh):
    in_specs = (P(("depth", "row"), "col"), P(("depth", "col"), "row"))
    out_specs = P(("row", "depth"), "col")
    return jax.shard_map(body, mesh=mesh, in_specs=in_specs, out_specs=out_specs, check_vma=False)
```

```python
import functools
import jax
import jax.numpy as jnp
from jax import lax
from jax.experimental import pallas as pl
from jax.experimental.pallas import tpu as pltpu
from jax.sharding import PartitionSpec as P

AXES = ("row", "col", "depth")
SIZES = (2, 4, 2, 4, 8)


def permute(value, target):
    pairs = []
    for zh in range(2):
        for x in range(4):
            for core in range(2):
                for y in range(4):
                    for zl in range(8):
                        to = target(zh, x, core, y, zl)
                        if to is not None:
                            flat = lambda c: ((((c[0] * 4 + c[1]) * 2 + c[2]) * 4 + c[3]) * 8 + c[4])
                            pairs.append((flat((zh, x, core, y, zl)), flat(to)))
    return lax.ppermute(value, AXES, pairs)


def over_x(value, step):
    return permute(value, lambda zh, x, c, y, zl: (zh, (x - step) % 4, c, y, zl))


def over_y(value, step):
    return permute(value, lambda zh, x, c, y, zl: (zh, x, c, (y - step) % 4, zl))


def other_core(value):
    return permute(value, lambda zh, x, c, y, zl: (zh, x, 1 - c, y, zl))


def other_half(value):
    return permute(value, lambda zh, x, c, y, zl: (1 - zh, x, c, y, zl))


def other_quad(value):
    return permute(value, lambda zh, x, c, y, zl: (zh, x, c, y, zl ^ 4))


def depth_pair(value, bit):
    return permute(value, lambda zh, x, c, y, zl: (zh, x, c, y, zl ^ bit))


NT = (((1,), (1,)), ((), ()))
TILES = ((0, 256), (256, 512), (512, 768), (768, 1024), (1024, 1136))
f16, f32, bf16 = jnp.float16, jnp.float32, jnp.bfloat16
PARAMS = pltpu.CompilerParams(vmem_limit_bytes=40 * 2**20)
VM = pl.BlockSpec(memory_space=pltpu.VMEM)
SM = pl.BlockSpec(memory_space=pltpu.SMEM)
ANY = pl.BlockSpec(memory_space=pl.ANY)


def cost(us):
    return pl.CostEstimate(flops=int(us * 1e9), bytes_accessed=2**20, transcendentals=0)


def shape(dims, dtype):
    return jax.ShapeDtypeStruct(dims, dtype)


def tie(*values):
    return lax.optimization_barrier(values)


def lanes_at(start, size):
    return pl.ds(pl.multiple_of(start, 128), size)


def fence_kernel(ref, out_ref):
    out_ref[...] = ref[...]


def prep_kernel(at_ref, all_ref, grads_ref, fetched, turned, sems):
    zh, zl = at_ref[0], at_ref[4]
    b0, b1, quad = lax.rem(zl, 2), lax.rem(zl // 2, 2), zl // 4
    copies = [pltpu.make_async_copy(all_ref.at[pl.ds(j * 512, 512), :], fetched.at[j], sems.at[j]) for j in range(4)]
    for copy in copies:
        copy.start()
    for j, copy in enumerate(copies):
        copy.wait()
        turned[...] = fetched[j].T
        slot = lax.rem(j - 2 * zh + 4, 4)
        for k in range(8):
            owner_quad = 1 - quad if k < 4 else quad
            owner_b0 = 1 - b0 if k % 4 < 2 else b0
            owner_b1 = 1 - b1 if k % 2 == 0 else b1
            first = (owner_quad * 4 + owner_b1 * 2 + owner_b0) * 96
            grads_ref[slot, k * 96:(k + 1) * 96, :] = turned[pl.ds(pl.multiple_of(first, 32), 96), :]


def spread(at_ref, own, other, acts_ref, sems):
    x, core = at_ref[1], at_ref[2]
    copies = []
    for xr in range(4):
        slot = lax.rem(x + xr, 4) * 256
        for i, (src, c) in enumerate(((own, core), (other, 1 - core))):
            copies.append(pltpu.make_async_copy(src.at[xr], acts_ref.at[:, lanes_at(slot + c * 128, 128)], sems.at[2 * xr + i]))
    for copy in copies:
        copy.start()
    return copies


def own_kernel(at_ref, s0, t0, grads_ref, token, out_ref, acts_ref, sems):
    for copy in spread(at_ref, s0, t0, acts_ref, sems):
        copy.wait()
    for lo, hi in TILES:
        out_ref[:, lo:hi] = sum(
            lax.dot_general(grads_ref[j], acts_ref[lo:hi, j * 512:(j + 1) * 512], NT, preferred_element_type=f32) for j in range(2))


def coded(total, size):
    total = total * jnp.exp2(7 - size)
    return total * jnp.abs(total)


def decoded(message, size):
    root = jnp.sqrt(jnp.abs(message)) * jnp.exp2(size - 7)
    return jnp.where(message < 0, -root, root)


def rest_kernel(at_ref, s1, t1, grads_ref, start_ref, *refs):
    far0_ref, far1_ref, near0_ref, near1_ref, keep_far_ref, keep_near_ref, acts_ref, sems = refs
    for copy in spread(at_ref, s1, t1, acts_ref, sems):
        copy.wait()
    places = ((far0_ref, 0), (far1_ref, 96), (keep_far_ref, 192), (near0_ref, 384), (near1_ref, 480), (keep_near_ref, 576))
    tops = []
    for lo, hi in TILES:
        part = start_ref[:, lo:hi] + sum(
            lax.dot_general(grads_ref[2 + j], acts_ref[lo:hi, j * 512:(j + 1) * 512], NT, preferred_element_type=f32) for j in range(2))
        for ref, first in places:
            ref[:, lo:hi] = part[first:first + ref.shape[0]]
        tops.append(jnp.max(jnp.abs(part), axis=1, keepdims=True))
    size = jnp.clip(jnp.ceil(jnp.log2(functools.reduce(jnp.maximum, tops))) + 1, -100, 100)
    for ref, first in places:
        rows = ref.shape[0]
        its = size[first:first + rows]
        ref[:, 1136:] = jnp.broadcast_to(its, (rows, 16))
        if rows == 96:
            ref[:, :1136] = coded(ref[:, :1136], its)


def stage_kernel(spans, keep_ref, message_ref, *out_refs):
    message = message_ref[...]
    size = message[:, 1136:1137]
    total = keep_ref[...] + decoded(message, size)
    size = jnp.maximum(keep_ref[:, 1136:1137], size) + 1
    lane = lax.broadcasted_iota(jnp.int32, total.shape, 1)
    kept = jnp.where(lane < 1136, total, size)
    sent = jnp.where(lane < 1136, coded(total, size), size)
    for (first, rows, on), ref in zip(spans, out_refs):
        ref[...] = (sent if on else kept)[first:first + rows]


def stage(keep, message, *spans):
    return pl.pallas_call(
        functools.partial(stage_kernel, spans), out_shape=tuple(shape((rows, 1152), f32) for _, rows, _ in spans),
        in_specs=[VM] * 2, out_specs=(VM,) * len(spans), compiler_params=PARAMS, name="stage",
    )(keep, message.astype(f32))


def final_kernel(near_ref, message_ref, out_ref):
    message = message_ref[...]
    out_ref[...] = (near_ref[...] + decoded(message, message[:, 1136:1137]))[:, :1136]


def again(token):
    return pl.pallas_call(
        fence_kernel, out_shape=shape((8, 128), f32), in_specs=[VM], out_specs=VM, compiler_params=PARAMS, name="fence",
    )(token)


def body(activations, out_grads):
    row, y, zl = (lax.axis_index(a) for a in AXES)
    where = jnp.stack([row // 8, row // 2 % 4, row % 2, y, zl]).astype(jnp.int32)
    bt = activations.T
    token = again(jnp.zeros((8, 128), f32) + row.astype(f32))
    every_grad = lax.all_gather(out_grads, "col", axis=0, tiled=True)
    bt, token = tie(bt, token)
    swapped = other_half(bt)
    x1, x2, x3 = (over_x(bt, s) for s in (1, 2, 3))
    swapped, token = tie(swapped, token)
    token = again(token)
    x1, x2, x3, swapped, token = tie(x1, x2, x3, swapped, token)
    s0 = jnp.stack([bt, x1, x2, x3])
    t0 = other_core(s0)
    o1, o2, o3 = (over_x(swapped, s) for s in (1, 2, 3))
    grads = pl.pallas_call(
        prep_kernel, out_shape=shape((4, 768, 512), bf16),
        in_specs=[SM, ANY], out_specs=VM, compiler_params=PARAMS, name="prep",
        scratch_shapes=[pltpu.VMEM((4, 512, 768), bf16), pltpu.VMEM((768, 512), bf16), pltpu.SemaphoreType.DMA((4,))],
    )(where, every_grad)
    o1, o2, o3, grads = tie(o1, o2, o3, grads)
    s1 = jnp.stack([swapped, o1, o2, o3])
    t1 = other_core(s1)
    t0, s1 = tie(t0, s1)
    start = pl.pallas_call(
        own_kernel, out_shape=shape((768, 1136), f32),
        in_specs=[SM] + [ANY] * 2 + [VM] * 2, out_specs=VM, compiler_params=PARAMS, name="own",
        scratch_shapes=[pltpu.VMEM((1136, 1024), bf16), pltpu.SemaphoreType.DMA((8,))],
    )(where, s0, t0, grads, token)
    t1, start = tie(t1, start)
    *sends, keep_far, keep_near = pl.pallas_call(
        rest_kernel, out_shape=(shape((96, 1152), f32),) * 4 + (shape((192, 1152), f32),) * 2,
        in_specs=[SM] + [ANY] * 2 + [VM] * 2, out_specs=(VM,) * 6, compiler_params=PARAMS, name="rest",
        scratch_shapes=[pltpu.VMEM((1136, 1024), bf16), pltpu.SemaphoreType.DMA((8,))],
    )(where, s1, t1, grads, start)
    f0, f1, n0, n1 = (depth_pair(m.astype(f16), 1) for m in sends)
    (f2,) = stage(keep_far[:96], f0, (0, 96, True))
    f2 = depth_pair(f2.astype(f16), 2)
    (far,) = stage(keep_far[96:], f1, (0, 96, False))
    (n2,) = stage(keep_near[:96], n0, (0, 96, True))
    n2 = depth_pair(n2.astype(f16), 2)
    crossed = depth_pair(stage(far, f2, (0, 96, True))[0].astype(f16), 4)
    (near,) = stage(keep_near[96:], n1, (0, 96, False))
    (near,) = stage(near, n2, (0, 96, False))
    near, crossed = tie(near, crossed)
    return pl.pallas_call(
        final_kernel, out_shape=shape((96, 1136), f32), in_specs=[VM] * 2, out_specs=VM, compiler_params=PARAMS, name="final",
    )(near, crossed.astype(f32))


def solution(mesh):
    in_specs = (P(("depth", "row"), "col"), P(("depth", "col"), "row"))
    out_specs = P(("row", "depth"), "col")
    return jax.shard_map(body, mesh=mesh, in_specs=in_specs, out_specs=out_specs, check_vma=False)
```

```python
import functools
import jax
import jax.numpy as jnp
from jax import lax
from jax.experimental import pallas as pl
from jax.experimental.pallas import tpu as pltpu
from jax.sharding import PartitionSpec as P

AXES = ("row", "col", "depth")
SIZES = (2, 4, 2, 4, 8)


def permute(value, target):
    pairs = []
    for zh in range(2):
        for x in range(4):
            for core in range(2):
                for y in range(4):
                    for zl in range(8):
                        to = target(zh, x, core, y, zl)
                        if to is not None:
                            flat = lambda c: ((((c[0] * 4 + c[1]) * 2 + c[2]) * 4 + c[3]) * 8 + c[4])
                            pairs.append((flat((zh, x, core, y, zl)), flat(to)))
    return lax.ppermute(value, AXES, pairs)


def over_x(value, step):
    return permute(value, lambda zh, x, c, y, zl: (zh, (x - step) % 4, c, y, zl))


def over_y(value, step):
    return permute(value, lambda zh, x, c, y, zl: (zh, x, c, (y - step) % 4, zl))


def other_core(value):
    return permute(value, lambda zh, x, c, y, zl: (zh, x, 1 - c, y, zl))


def other_half(value):
    return permute(value, lambda zh, x, c, y, zl: (1 - zh, x, c, y, zl))


def other_quad(value):
    return permute(value, lambda zh, x, c, y, zl: (zh, x, c, y, zl ^ 4))


def depth_pair(value, bit):
    return permute(value, lambda zh, x, c, y, zl: (zh, x, c, y, zl ^ bit))


NT = (((1,), (1,)), ((), ()))
TILES = ((0, 256), (256, 512), (512, 768), (768, 1024), (1024, 1136))
f16, f32, bf16 = jnp.float16, jnp.float32, jnp.bfloat16
PARAMS = pltpu.CompilerParams(vmem_limit_bytes=40 * 2**20)
VM = pl.BlockSpec(memory_space=pltpu.VMEM)
SM = pl.BlockSpec(memory_space=pltpu.SMEM)
ANY = pl.BlockSpec(memory_space=pl.ANY)


def cost(us):
    return pl.CostEstimate(flops=int(us * 1e9), bytes_accessed=2**20, transcendentals=0)


def shape(dims, dtype):
    return jax.ShapeDtypeStruct(dims, dtype)


def tie(*values):
    return lax.optimization_barrier(values)


def lanes_at(start, size):
    return pl.ds(pl.multiple_of(start, 128), size)


def fence_kernel(ref, out_ref):
    out_ref[...] = ref[...]


def prep_kernel(at_ref, all_ref, grads_ref, fetched, turned, sems):
    zh, zl = at_ref[0], at_ref[4]
    b0, b1, quad = lax.rem(zl, 2), lax.rem(zl // 2, 2), zl // 4
    copies = [pltpu.make_async_copy(all_ref.at[pl.ds(j * 512, 512), :], fetched.at[j], sems.at[j]) for j in range(4)]
    for copy in copies:
        copy.start()
    for j, copy in enumerate(copies):
        copy.wait()
        turned[...] = fetched[j].T
        slot = lax.rem(j - 2 * zh + 4, 4)
        for k in range(8):
            owner_quad = 1 - quad if k < 4 else quad
            owner_b0 = 1 - b0 if k % 4 < 2 else b0
            owner_b1 = 1 - b1 if k % 2 == 0 else b1
            first = (owner_quad * 4 + owner_b1 * 2 + owner_b0) * 96
            grads_ref[slot, k * 96:(k + 1) * 96, :] = turned[pl.ds(pl.multiple_of(first, 32), 96), :]


def spread(at_ref, own, other, acts_ref, sems, lo=0, hi=1136, sem=0):
    x, core = at_ref[1], at_ref[2]
    copies = []
    for xr in range(4):
        slot = lax.rem(x + xr, 4) * 256
        for i, (src, c) in enumerate(((own, core), (other, 1 - core))):
            copies.append(pltpu.make_async_copy(
                src.at[xr, lo:hi, :], acts_ref.at[lo:hi, lanes_at(slot + c * 128, 128)], sems.at[sem + 2 * xr + i]))
    for copy in copies:
        copy.start()
    return copies


def own_kernel(at_ref, s0, t0, grads_ref, token, out_ref, acts_ref, sems):
    for copy in spread(at_ref, s0, t0, acts_ref, sems):
        copy.wait()
    for lo, hi in TILES:
        out_ref[:, lo:hi] = sum(
            lax.dot_general(grads_ref[j], acts_ref[lo:hi, j * 512:(j + 1) * 512], NT, preferred_element_type=f32) for j in range(2))


def coded(total, size):
    total = total * jnp.exp2(7 - size)
    return total * jnp.abs(total)


def decoded(message, size):
    root = jnp.sqrt(jnp.abs(message)) * jnp.exp2(size - 7)
    return jnp.where(message < 0, -root, root)


def rest_kernel(at_ref, s1, t1, grads_ref, start_ref, *refs):
    far0_ref, far1_ref, near0_ref, near1_ref, keep_far_ref, keep_near_ref, acts_ref, sems = refs
    arriving = [spread(at_ref, s1, t1, acts_ref, sems, lo, hi, 8 * i) for i, (lo, hi) in enumerate(TILES)]
    places = ((far0_ref, 0), (far1_ref, 96), (keep_far_ref, 192), (near0_ref, 384), (near1_ref, 480), (keep_near_ref, 576))
    tops = []
    for (lo, hi), copies in zip(TILES, arriving):
        for copy in copies:
            copy.wait()
        part = start_ref[:, lo:hi] + sum(
            lax.dot_general(grads_ref[2 + j], acts_ref[lo:hi, j * 512:(j + 1) * 512], NT, preferred_element_type=f32) for j in range(2))
        for ref, first in places:
            ref[:, lo:hi] = part[first:first + ref.shape[0]]
        tops.append(jnp.max(jnp.abs(part), axis=1, keepdims=True))
    size = jnp.clip(jnp.ceil(jnp.log2(functools.reduce(jnp.maximum, tops))) + 1, -100, 100)
    for ref, first in places:
        rows = ref.shape[0]
        its = size[first:first + rows]
        ref[:, 1136:] = jnp.broadcast_to(its, (rows, 16))
        if rows == 96:
            ref[:, :1136] = coded(ref[:, :1136], its)


def stage_kernel(spans, keep_ref, message_ref, *out_refs):
    message = message_ref[...]
    size = message[:, 1136:1137]
    total = keep_ref[...] + decoded(message, size)
    size = jnp.maximum(keep_ref[:, 1136:1137], size) + 1
    lane = lax.broadcasted_iota(jnp.int32, total.shape, 1)
    kept = jnp.where(lane < 1136, total, size)
    sent = jnp.where(lane < 1136, coded(total, size), size)
    for (first, rows, on), ref in zip(spans, out_refs):
        ref[...] = (sent if on else kept)[first:first + rows]


def stage(keep, message, *spans):
    return pl.pallas_call(
        functools.partial(stage_kernel, spans), out_shape=tuple(shape((rows, 1152), f32) for _, rows, _ in spans),
        in_specs=[VM] * 2, out_specs=(VM,) * len(spans), compiler_params=PARAMS, name="stage",
    )(keep, message.astype(f32))


def final_kernel(near_ref, message_ref, out_ref):
    message = message_ref[...]
    out_ref[...] = (near_ref[...] + decoded(message, message[:, 1136:1137]))[:, :1136]


def again(token):
    return pl.pallas_call(
        fence_kernel, out_shape=shape((8, 128), f32), in_specs=[VM], out_specs=VM, compiler_params=PARAMS, name="fence",
    )(token)


def body(activations, out_grads):
    row, y, zl = (lax.axis_index(a) for a in AXES)
    where = jnp.stack([row // 8, row // 2 % 4, row % 2, y, zl]).astype(jnp.int32)
    bt = activations.T
    token = again(jnp.zeros((8, 128), f32) + row.astype(f32))
    every_grad = lax.all_gather(out_grads, "col", axis=0, tiled=True)
    bt, token = tie(bt, token)
    swapped = other_half(bt)
    x1, x2, x3 = (over_x(bt, s) for s in (1, 2, 3))
    swapped, token = tie(swapped, token)
    token = again(token)
    x1, x2, x3, swapped, token = tie(x1, x2, x3, swapped, token)
    s0 = jnp.stack([bt, x1, x2, x3])
    t0 = other_core(s0)
    o2, o1, o3 = (over_x(swapped, s) for s in (2, 1, 3))
    grads = pl.pallas_call(
        prep_kernel, out_shape=shape((4, 768, 512), bf16),
        in_specs=[SM, ANY], out_specs=VM, compiler_params=PARAMS, name="prep",
        scratch_shapes=[pltpu.VMEM((4, 512, 768), bf16), pltpu.VMEM((768, 512), bf16), pltpu.SemaphoreType.DMA((4,))],
    )(where, every_grad)
    o2, o1, o3, grads = tie(o2, o1, o3, grads)
    s1 = jnp.stack([swapped, o1, o2, o3])
    t1 = other_core(s1)
    t0, s1 = tie(t0, s1)
    start = pl.pallas_call(
        own_kernel, out_shape=shape((768, 1136), f32),
        in_specs=[SM] + [ANY] * 2 + [VM] * 2, out_specs=VM, compiler_params=PARAMS, name="own",
        scratch_shapes=[pltpu.VMEM((1136, 1024), bf16), pltpu.SemaphoreType.DMA((8,))],
    )(where, s0, t0, grads, token)
    t1, start = tie(t1, start)
    *sends, keep_far, keep_near = pl.pallas_call(
        rest_kernel, out_shape=(shape((96, 1152), f32),) * 4 + (shape((192, 1152), f32),) * 2,
        in_specs=[SM] + [ANY] * 2 + [VM] * 2, out_specs=(VM,) * 6, compiler_params=PARAMS, name="rest",
        scratch_shapes=[pltpu.VMEM((1136, 1024), bf16), pltpu.SemaphoreType.DMA((40,))],
    )(where, s1, t1, grads, start)
    f0, f1, n0, n1 = (depth_pair(m.astype(f16), 1) for m in sends)
    (f2,) = stage(keep_far[:96], f0, (0, 96, True))
    f2 = depth_pair(f2.astype(f16), 2)
    (far,) = stage(keep_far[96:], f1, (0, 96, False))
    (n2,) = stage(keep_near[:96], n0, (0, 96, True))
    n2 = depth_pair(n2.astype(f16), 2)
    crossed = depth_pair(stage(far, f2, (0, 96, True))[0].astype(f16), 4)
    (near,) = stage(keep_near[96:], n1, (0, 96, False))
    (near,) = stage(near, n2, (0, 96, False))
    near, crossed = tie(near, crossed)
    return pl.pallas_call(
        final_kernel, out_shape=shape((96, 1136), f32), in_specs=[VM] * 2, out_specs=VM, compiler_params=PARAMS, name="final",
    )(near, crossed.astype(f32))


def solution(mesh):
    in_specs = (P(("depth", "row"), "col"), P(("depth", "col"), "row"))
    out_specs = P(("row", "depth"), "col")
    return jax.shard_map(body, mesh=mesh, in_specs=in_specs, out_specs=out_specs, check_vma=False)
```

```python
import functools
import jax
import jax.numpy as jnp
from jax import lax
from jax.experimental import pallas as pl
from jax.experimental.pallas import tpu as pltpu
from jax.sharding import PartitionSpec as P

AXES = ("row", "col", "depth")
SIZES = (2, 4, 2, 4, 8)


def permute(value, target):
    pairs = []
    for zh in range(2):
        for x in range(4):
            for core in range(2):
                for y in range(4):
                    for zl in range(8):
                        to = target(zh, x, core, y, zl)
                        if to is not None:
                            flat = lambda c: ((((c[0] * 4 + c[1]) * 2 + c[2]) * 4 + c[3]) * 8 + c[4])
                            pairs.append((flat((zh, x, core, y, zl)), flat(to)))
    return lax.ppermute(value, AXES, pairs)


def over_x(value, step):
    return permute(value, lambda zh, x, c, y, zl: (zh, (x - step) % 4, c, y, zl))


def over_y(value, step):
    return permute(value, lambda zh, x, c, y, zl: (zh, x, c, (y - step) % 4, zl))


def other_core(value):
    return permute(value, lambda zh, x, c, y, zl: (zh, x, 1 - c, y, zl))


def other_half(value):
    return permute(value, lambda zh, x, c, y, zl: (1 - zh, x, c, y, zl))


def other_quad(value):
    return permute(value, lambda zh, x, c, y, zl: (zh, x, c, y, zl ^ 4))


def depth_pair(value, bit):
    return permute(value, lambda zh, x, c, y, zl: (zh, x, c, y, zl ^ bit))


NT = (((1,), (1,)), ((), ()))
TILES = ((0, 256), (256, 512), (512, 768), (768, 1024), (1024, 1136))
f16, f32, bf16 = jnp.float16, jnp.float32, jnp.bfloat16
PARAMS = pltpu.CompilerParams(vmem_limit_bytes=40 * 2**20)
VM = pl.BlockSpec(memory_space=pltpu.VMEM)
SM = pl.BlockSpec(memory_space=pltpu.SMEM)
ANY = pl.BlockSpec(memory_space=pl.ANY)


def cost(us):
    return pl.CostEstimate(flops=int(us * 1e9), bytes_accessed=2**20, transcendentals=0)


def shape(dims, dtype):
    return jax.ShapeDtypeStruct(dims, dtype)


def tie(*values):
    return lax.optimization_barrier(values)


def lanes_at(start, size):
    return pl.ds(pl.multiple_of(start, 128), size)


def fence_kernel(ref, out_ref):
    out_ref[...] = ref[...]


def prep_kernel(at_ref, all_ref, grads_ref, fetched, turned, sems):
    zh, zl = at_ref[0], at_ref[4]
    b0, b1, quad = lax.rem(zl, 2), lax.rem(zl // 2, 2), zl // 4
    copies = [pltpu.make_async_copy(all_ref.at[pl.ds(j * 512, 512), :], fetched.at[j], sems.at[j]) for j in range(4)]
    for copy in copies:
        copy.start()
    for j, copy in enumerate(copies):
        copy.wait()
        turned[...] = fetched[j].T
        slot = lax.rem(j - 2 * zh + 4, 4)
        for k in range(8):
            owner_quad = 1 - quad if k < 4 else quad
            owner_b0 = 1 - b0 if k % 4 < 2 else b0
            owner_b1 = 1 - b1 if k % 2 == 0 else b1
            first = (owner_quad * 4 + owner_b1 * 2 + owner_b0) * 96
            grads_ref[slot, k * 96:(k + 1) * 96, :] = turned[pl.ds(pl.multiple_of(first, 32), 96), :]


def spread(at_ref, own, other, acts_ref, sems):
    x, core = at_ref[1], at_ref[2]
    copies = []
    for xr in range(4):
        slot = lax.rem(x + xr, 4) * 256
        for i, (src, c) in enumerate(((own, core), (other, 1 - core))):
            copies.append(pltpu.make_async_copy(src.at[xr], acts_ref.at[:, lanes_at(slot + c * 128, 128)], sems.at[2 * xr + i]))
    for copy in copies:
        copy.start()
    return copies


def own_kernel(at_ref, s0, t0, grads_ref, token, out_ref, acts_ref, sems):
    for copy in spread(at_ref, s0, t0, acts_ref, sems):
        copy.wait()
    for lo, hi in TILES:
        out_ref[:, lo:hi] = sum(
            lax.dot_general(grads_ref[j], acts_ref[lo:hi, j * 512:(j + 1) * 512], NT, preferred_element_type=f32) for j in range(2))


def coded(total, size):
    total = total * jnp.exp2(7 - size)
    return total * jnp.abs(total)


def decoded(message, size):
    root = jnp.sqrt(jnp.abs(message)) * jnp.exp2(size - 7)
    return jnp.where(message < 0, -root, root)


def rest_kernel(at_ref, s1, t1, grads_ref, start_ref, *refs):
    far0_ref, far1_ref, near0_ref, near1_ref, keep_far_ref, keep_near_ref, acts_ref, sems = refs
    for copy in spread(at_ref, s1, t1, acts_ref, sems):
        copy.wait()
    places = ((far0_ref, 0), (far1_ref, 96), (keep_far_ref, 192), (near0_ref, 384), (near1_ref, 480), (keep_near_ref, 576))
    tops = []
    for lo, hi in TILES:
        part = start_ref[:, lo:hi] + sum(
            lax.dot_general(grads_ref[2 + j], acts_ref[lo:hi, j * 512:(j + 1) * 512], NT, preferred_element_type=f32) for j in range(2))
        for ref, first in places:
            ref[:, lo:hi] = part[first:first + ref.shape[0]]
        tops.append(jnp.max(jnp.abs(part), axis=1, keepdims=True))
    size = jnp.clip(jnp.ceil(jnp.log2(functools.reduce(jnp.maximum, tops))) + 1, -100, 100)
    for ref, first in places:
        rows = ref.shape[0]
        its = size[first:first + rows]
        ref[:, 1136:] = jnp.broadcast_to(its, (rows, 16))
        if rows == 96:
            ref[:, :1136] = coded(ref[:, :1136], its)


def stage_kernel(spans, keep_ref, message_ref, *out_refs):
    message = message_ref[...]
    size = message[:, 1136:1137]
    total = keep_ref[...] + decoded(message, size)
    size = jnp.maximum(keep_ref[:, 1136:1137], size) + 1
    lane = lax.broadcasted_iota(jnp.int32, total.shape, 1)
    kept = jnp.where(lane < 1136, total, size)
    sent = jnp.where(lane < 1136, coded(total, size), size)
    for (first, rows, on), ref in zip(spans, out_refs):
        ref[...] = (sent if on else kept)[first:first + rows]


def stage(keep, message, *spans):
    return pl.pallas_call(
        functools.partial(stage_kernel, spans), out_shape=tuple(shape((rows, 1152), f32) for _, rows, _ in spans),
        in_specs=[VM] * 2, out_specs=(VM,) * len(spans), compiler_params=PARAMS, name="stage",
    )(keep, message.astype(f32))


def final_kernel(near_ref, message_ref, out_ref):
    message = message_ref[...]
    out_ref[...] = (near_ref[...] + decoded(message, message[:, 1136:1137]))[:, :1136]


def again(token):
    return pl.pallas_call(
        fence_kernel, out_shape=shape((8, 128), f32), in_specs=[VM], out_specs=VM, compiler_params=PARAMS, name="fence",
    )(token)


def body(activations, out_grads):
    row, y, zl = (lax.axis_index(a) for a in AXES)
    where = jnp.stack([row // 8, row // 2 % 4, row % 2, y, zl]).astype(jnp.int32)
    bt = activations.T
    token = again(jnp.zeros((8, 128), f32) + row.astype(f32))
    every_grad = lax.all_gather(out_grads, "col", axis=0, tiled=True)
    bt, token = tie(bt, token)
    swapped = other_half(bt)
    x1, x2, x3 = (over_x(bt, s) for s in (1, 2, 3))
    swapped, token = tie(swapped, token)
    token = again(token)
    x1, x2, x3, swapped, token = tie(x1, x2, x3, swapped, token)
    s0 = jnp.stack([bt, x1, x2, x3])
    t0 = other_core(s0)
    o1, o2, o3 = (over_x(swapped, s) for s in (1, 2, 3))
    grads = pl.pallas_call(
        prep_kernel, out_shape=shape((4, 768, 512), bf16),
        in_specs=[SM, pl.BlockSpec(memory_space=pltpu.HBM)], out_specs=VM, compiler_params=PARAMS, name="prep",
        scratch_shapes=[pltpu.VMEM((4, 512, 768), bf16), pltpu.VMEM((768, 512), bf16), pltpu.SemaphoreType.DMA((4,))],
    )(where, every_grad)
    o1, o2, o3, grads = tie(o1, o2, o3, grads)
    s1 = jnp.stack([swapped, o1, o2, o3])
    t1 = other_core(s1)
    t0, s1 = tie(t0, s1)
    start = pl.pallas_call(
        own_kernel, out_shape=shape((768, 1136), f32),
        in_specs=[SM] + [ANY] * 2 + [VM] * 2, out_specs=VM, compiler_params=PARAMS, name="own",
        scratch_shapes=[pltpu.VMEM((1136, 1024), bf16), pltpu.SemaphoreType.DMA((8,))],
    )(where, s0, t0, grads, token)
    t1, start = tie(t1, start)
    *sends, keep_far, keep_near = pl.pallas_call(
        rest_kernel, out_shape=(shape((96, 1152), f32),) * 4 + (shape((192, 1152), f32),) * 2,
        in_specs=[SM] + [ANY] * 2 + [VM] * 2, out_specs=(VM,) * 6, compiler_params=PARAMS, name="rest",
        scratch_shapes=[pltpu.VMEM((1136, 1024), bf16), pltpu.SemaphoreType.DMA((8,))],
    )(where, s1, t1, grads, start)
    f0, f1, n0, n1 = (depth_pair(m.astype(f16), 1) for m in sends)
    (f2,) = stage(keep_far[:96], f0, (0, 96, True))
    f2 = depth_pair(f2.astype(f16), 2)
    (far,) = stage(keep_far[96:], f1, (0, 96, False))
    (n2,) = stage(keep_near[:96], n0, (0, 96, True))
    n2 = depth_pair(n2.astype(f16), 2)
    crossed = depth_pair(stage(far, f2, (0, 96, True))[0].astype(f16), 4)
    (near,) = stage(keep_near[96:], n1, (0, 96, False))
    (near,) = stage(near, n2, (0, 96, False))
    near, crossed = tie(near, crossed)
    return pl.pallas_call(
        final_kernel, out_shape=shape((96, 1136), f32), in_specs=[VM] * 2, out_specs=VM, compiler_params=PARAMS, name="final",
    )(near, crossed.astype(f32))


def solution(mesh):
    in_specs = (P(("depth", "row"), "col"), P(("depth", "col"), "row"))
    out_specs = P(("row", "depth"), "col")
    return jax.shard_map(body, mesh=mesh, in_specs=in_specs, out_specs=out_specs, check_vma=False)
```
